32 devices in a mesh: groups: 2 (over y), mp: 8 (over z, x), dp: 2 (over core).
Axes of the slice: x: 2, y: 2, z: 4, core: 2. Of those that a mesh axis runs over, the one named last changes fastest.
Arguments:
- queries: bfloat16 [4, 1024, 2048], P(('groups', 'dp'), 'mp'), parts along dimension 0
- keys: bfloat16 [4, 1024, 2048], P(('groups', 'dp'), 'mp'), parts along dimension 0
- values: bfloat16 [4, 1024, 2048], P(('groups', 'dp'), 'mp'), parts along dimension 0, may hold values from -6 to 6
- grad_out: bfloat16 [4, 1024, 2048], P(('groups', 'dp'), 'mp'), parts along dimension 0, may hold values from -6 to 6
- neighbours: int32 [4, 8, 4], P(('groups', 'dp'), 'mp'), parts along dimension 0, may hold values from -1 to 7, as said below
- counts: int32 [4, 8], P(('groups', 'dp'), 'mp'), parts along dimension 0, may hold values from 1 to 4, as said below
Outputs:
- attended: bfloat16 [4, 1024, 2048], P(('groups', 'dp'), 'mp'), parts along dimension 0
- grad_queries: bfloat16 [4, 1024, 2048], P(('groups', 'dp'), 'mp'), parts along dimension 0
- grad_keys: bfloat16 [4, 1024, 2048], P(('groups', 'dp'), 'mp'), parts along dimension 0
- grad_values: bfloat16 [4, 1024, 2048], P(('groups', 'dp'), 'mp'), parts along dimension 0
The draws below stay inside these ranges and needn't reach their ends.
There are 2 independent parts, one for each index of `groups`. The reference program is written for one: setup_inputs(seed, part) draws one part's arguments, and reference() takes and returns one part's arrays. A program takes and returns all parts, laid end to end along the dimension named above; each array names one. Nothing has to cross between parts.
Inputs may be any that keep to these rules, and one draw needn't show every extreme that they name: The first counts[b, t] entries of neighbours[b, t, :] are distinct tiles t + o of the same row with 1 <= |o| <= 2; the other entries are -1. `counts`: every row has a tile with 4 listed tiles and a tile with one.
All inputs are finite; a program needn't handle non-finite values.
Results may differ from the reference program's by a relative error of at most 0.0085.
Values may be sent and summed in bfloat16 or wider, within the bound.
A program may use at most 64 MiB of HBM per device.

```python
import jax
import jax.numpy as jnp
from jax import lax

HEADS = 16
HEAD_DIM = 128
TILE = 128
REACH = 2
MAXN = 4
MODEL = 2048
BATCH = 2
NTILE = 8
SEG = 1024


def token_common(key):
    return jax.random.normal(key, (BATCH, SEG, HEADS * HEAD_DIM), jnp.float32)


def tile_graph(key):
    pick_key, count_one, count_two, place_key = jax.random.split(key, 4)
    tile_ids = jnp.arange(NTILE, dtype=jnp.int32)[None, :]
    offsets = jnp.concatenate([jnp.arange(-REACH, 0, dtype=jnp.int32), jnp.arange(1, REACH + 1, dtype=jnp.int32)])
    target = tile_ids[:, :, None] + offsets[None, None, :]
    inside = (target >= 0) & (target < NTILE)
    available = jnp.sum(inside.astype(jnp.int32), axis=-1)
    places = jnp.arange(MAXN, dtype=jnp.int32)
    scores = jax.random.randint(pick_key, (BATCH, NTILE, MAXN), 0, 1 << 20) * MAXN + places
    scores = jnp.where(inside, scores, (1 << 22) * MAXN + places)
    forced = (tile_ids[:, :, None] == NTILE - 2) & (target == NTILE - 1)
    scores = jnp.where(forced, places - MAXN, scores)
    order = jnp.argsort(scores, axis=-1)
    chosen = jnp.take_along_axis(jnp.broadcast_to(target, (BATCH, NTILE, MAXN)), order, axis=-1)
    listed_count = 1 + jax.random.randint(count_one, (BATCH, NTILE), 0, MAXN) * jax.random.randint(count_two, (BATCH, NTILE), 0, MAXN) // MAXN
    listed_count = jnp.minimum(listed_count, available)
    busiest = jax.random.randint(place_key, (BATCH, 1), REACH, NTILE - REACH)
    listed_count = jnp.where(tile_ids == busiest, MAXN, listed_count)
    listed_count = jnp.where(tile_ids == busiest + 1, 1, listed_count)
    listed = jnp.where(places[None, None, :] < listed_count[:, :, None], chosen, -1)
    return (listed.astype(jnp.int32), listed_count.astype(jnp.int32))


def draw_neighbours(key, part):
    listed, listed_count = tile_graph(key)
    return listed


def draw_counts(key, part):
    listed, listed_count = tile_graph(key)
    return listed_count


def draw_queries(key, part):
    common = token_common(key)
    key = jax.random.fold_in(key, 11)
    first_key = jax.random.fold_in(key, 0)
    sample = jax.random.normal(first_key, common.shape, jnp.float32)
    return sample.astype(jnp.bfloat16)


def draw_keys(key, part):
    common = token_common(key)
    key = jax.random.fold_in(key, 12)
    first_key = jax.random.fold_in(key, 0)
    sample = jax.random.normal(first_key, common.shape, jnp.float32)
    return sample.astype(jnp.bfloat16)


def steps_of(key, dims, shards, low, largest):
    def one(axis_at, parts):
        heights = jax.random.uniform(jax.random.fold_in(jax.random.fold_in(key, 6), axis_at), (parts,), jnp.float32, low / len(shards), largest / len(shards))
        return jnp.repeat(jnp.exp(heights), dims[axis_at] // parts).reshape((-1,) + (1,) * (len(dims) - axis_at - 1))

    level = one(*shards[0])
    for cut in shards[1:]:
        level = level * one(*cut)
    return level


def scatter_about(rng, extent, scale, bound, cuts=(), held_as=jnp.bfloat16):
    array = scale * jax.random.normal(rng, extent, jnp.float32)
    if cuts:
        array = array * steps_of(rng, extent, cuts, -0.22, 0.18)
    return jnp.clip(array, -bound, bound).astype(held_as)


def setup_inputs(seed: int = 0, part: int = 0) -> dict:
    splits = jax.random.split(jax.random.key(seed), 7)
    part_keys = jax.random.split(jax.random.fold_in(splits[6], part), 7)
    return {
        "queries": draw_queries(jax.random.fold_in(jax.random.fold_in(splits[6], part), 71), part),
        "keys": draw_keys(jax.random.fold_in(jax.random.fold_in(splits[6], part), 71), part),
        "values": scatter_about(part_keys[2], (BATCH, SEG, MODEL), 1.0, 6.0, ((0, 2), (1, 8))),
        "grad_out": scatter_about(part_keys[3], (BATCH, SEG, MODEL), 1.0, 6.0, ((0, 2), (1, 8))),
        "neighbours": draw_neighbours(jax.random.fold_in(jax.random.fold_in(splits[6], part), 71), part),
        "counts": draw_counts(jax.random.fold_in(jax.random.fold_in(splits[6], part), 71), part),
    }


def tile_step(query, key_block, value_block, grad_tile, present):
    inv_root = HEAD_DIM ** -0.5
    window_size = 2 * REACH + 1
    query_heads = query.astype(jnp.float32).reshape(TILE, HEADS, HEAD_DIM)
    key_heads = key_block.astype(jnp.float32).reshape(window_size * TILE, HEADS, HEAD_DIM)
    value_heads = value_block.astype(jnp.float32).reshape(window_size * TILE, HEADS, HEAD_DIM)
    grad_heads = grad_tile.astype(jnp.float32).reshape(TILE, HEADS, HEAD_DIM)
    scores = jnp.einsum('qhe,khe->hqk', query_heads, key_heads) * inv_root
    keymask = jnp.repeat(present, TILE)
    scores = jnp.where(keymask[None, None, :], scores, -jnp.inf)
    row_max = jnp.max(scores, axis=-1, keepdims=True)
    exponent = jnp.exp(scores - row_max)
    weights = exponent / jnp.sum(exponent, axis=-1, keepdims=True)
    weights_low = lax.optimization_barrier(weights.astype(jnp.bfloat16)).astype(jnp.float32)
    mixture = jnp.einsum('hqk,khe->qhe', weights_low, value_heads)
    grad_prob = jnp.einsum('qhe,khe->hqk', grad_heads, value_heads)
    row_delta = jnp.transpose(jnp.sum(grad_heads * mixture, axis=-1))[:, :, None]
    dscore = lax.optimization_barrier((weights * (grad_prob - row_delta) * inv_root).astype(jnp.bfloat16)).astype(jnp.float32)
    grad_query = jnp.einsum('hqk,khe->qhe', dscore, key_heads)
    key_share = jnp.einsum('hqk,qhe->khe', dscore, query_heads).reshape(window_size * TILE, HEADS * HEAD_DIM)
    value_share = jnp.einsum('hqk,qhe->khe', weights_low, grad_heads).reshape(window_size * TILE, HEADS * HEAD_DIM)
    return mixture.reshape(TILE, HEADS * HEAD_DIM), grad_query.reshape(TILE, HEADS * HEAD_DIM), key_share, value_share


def reference(queries, keys, values, grad_out, neighbours, counts):
    window_size = 2 * REACH + 1
    margin = REACH * TILE
    features = HEADS * HEAD_DIM
    offsets = jnp.arange(-REACH, REACH + 1, dtype=jnp.int32)
    places = jnp.arange(MAXN, dtype=jnp.int32)
    attended_rows, grad_q_rows, grad_k_rows, grad_v_rows = [], [], [], []
    for row_idx in range(BATCH):
        key_pad = jnp.pad(keys[row_idx], ((margin, margin), (0, 0)))
        value_pad = jnp.pad(values[row_idx], ((margin, margin), (0, 0)))
        row_queries = queries[row_idx]
        row_grads = grad_out[row_idx]
        row_lists = neighbours[row_idx]
        row_counts = counts[row_idx]

        def step(carry, tile_idx):
            key_acc, value_acc = carry
            start = tile_idx * TILE
            query = lax.dynamic_slice_in_dim(row_queries, start, TILE, 0)
            grad_tile = lax.dynamic_slice_in_dim(row_grads, start, TILE, 0)
            key_block = lax.dynamic_slice_in_dim(key_pad, start, window_size * TILE, 0)
            value_block = lax.dynamic_slice_in_dim(value_pad, start, window_size * TILE, 0)
            listed = row_lists[tile_idx]
            listed_count = row_counts[tile_idx]
            present = jnp.any((listed[None, :] == tile_idx + offsets[:, None]) & (places[None, :] < listed_count), axis=1) | (offsets == 0)
            mixture, grad_query, key_share, value_share = tile_step(query, key_block, value_block, grad_tile, present)
            key_share = lax.optimization_barrier(key_share.astype(jnp.bfloat16)).astype(jnp.float32)
            value_share = lax.optimization_barrier(value_share.astype(jnp.bfloat16)).astype(jnp.float32)
            key_acc = lax.dynamic_update_slice_in_dim(key_acc, lax.dynamic_slice_in_dim(key_acc, start, window_size * TILE, 0) + key_share, start, 0)
            value_acc = lax.dynamic_update_slice_in_dim(value_acc, lax.dynamic_slice_in_dim(value_acc, start, window_size * TILE, 0) + value_share, start, 0)
            return (key_acc, value_acc), (mixture.astype(jnp.bfloat16), grad_query.astype(jnp.bfloat16))

        zeros_acc = jnp.zeros((SEG + 2 * margin, features), jnp.float32)
        (key_acc, value_acc), (mixed_rows, grad_rows) = lax.scan(step, (zeros_acc, zeros_acc), jnp.arange(NTILE, dtype=jnp.int32))
        attended_rows.append(mixed_rows.reshape(SEG, features))
        grad_q_rows.append(grad_rows.reshape(SEG, features))
        grad_k_rows.append(key_acc[margin:margin + SEG].astype(jnp.bfloat16))
        grad_v_rows.append(value_acc[margin:margin + SEG].astype(jnp.bfloat16))
    return (jnp.stack(attended_rows), jnp.stack(grad_q_rows), jnp.stack(grad_k_rows), jnp.stack(grad_v_rows))
```

```python
import functools

import jax
import jax.numpy as jnp
from jax import lax
from jax.experimental import pallas as pl
from jax.experimental.pallas import tpu as pltpu
from jax.sharding import PartitionSpec as P

HEADS = 16
HEAD_DIM = 128
TILE = 128
REACH = 2
MAXN = 4
HALF = HEADS // 2
SLOTS = 6
AHEAD = 2
BEHIND = 1
INV_ROOT = HEAD_DIM ** (-0.5)
MESH = pl.DeviceIdType.MESH


def nt(a, b):
    return lax.dot_general(a, b, (((1,), (1,)), ((), ())), preferred_element_type=jnp.float32)


def nn(a, b):
    return jnp.dot(a, b, preferred_element_type=jnp.float32)


def kernel(
    peers,
    neighbours_ref, counts_ref, q_ref, k_ref, v_ref, g_ref,
    att_ref, gq_ref, gk_ref, gv_ref,
    kv, qg, share_out, share_in, result, own, bias,
    send_sem, recv_sem, local_sem, bias_sem,
):
    me = lax.axis_index("mp")
    side = lax.rem(me, 2)
    other = 1 - side
    partner = me + 1 - 2 * side
    pair = lax.div(me, 2)
    has_up = me + 2 < peers
    has_down = me >= 2
    up = me + 2
    down = me - 2
    width = HALF * HEAD_DIM

    def columns(half, h):
        return pl.ds(pl.multiple_of(half * width + h * HEAD_DIM, HEAD_DIM), HEAD_DIM)

    def remote(src, dst, stream, h, target):
        return pltpu.make_async_remote_copy(
            src_ref=src,
            dst_ref=dst,
            send_sem=send_sem.at[h, stream],
            recv_sem=recv_sem.at[h, stream],
            device_id={"mp": target},
            device_id_type=MESH,
        )

    inputs = (k_ref, v_ref, q_ref, g_ref)
    outputs = (att_ref, gq_ref, gk_ref, gv_ref)

    def place(i, h, which):
        return kv.at[h, 1, which, i] if i < 2 else qg.at[h, which, i - 2]

    def give(i, h):
        return remote(
            inputs[i].at[0, :, columns(other, h)], place(i, h, side), i, h, partner
        )

    def take(i, h):
        return remote(
            inputs[i].at[0, :, columns(other, h)], place(i, h, other), i, h, partner
        )

    def keep(i, h):
        return pltpu.make_async_copy(
            inputs[i].at[0, :, columns(side, h)], place(i, h, side), local_sem.at[h, i]
        )

    def own_up(i, h):
        return remote(inputs[i].at[0, :, columns(side, h)], kv.at[h, 0, side, i], 4 + i, h, up)

    def own_down(i, h):
        return remote(inputs[i].at[0, :, columns(side, h)], kv.at[h, 2, side, i], 6 + i, h, down)

    def pass_up(h):
        return remote(kv.at[h, 1, other], kv.at[h, 0, other], 8, h, up)

    def pass_down(h):
        return remote(kv.at[h, 1, other], kv.at[h, 2, other], 9, h, down)

    def share_up(h):
        return remote(share_out.at[h, 1], share_in.at[h, 0], 10, h, up)

    def share_down(h):
        return remote(share_out.at[h, 0], share_in.at[h, 1], 11, h, down)

    def hand_back(i, h):
        return remote(
            result.at[h, other, i], outputs[i].at[0, :, columns(side, h)], 12 + i, h, partner
        )

    def take_back(i, h):
        return remote(
            result.at[h, other, i], outputs[i].at[0, :, columns(other, h)], 12 + i, h, partner
        )

    def write(i, h):
        return pltpu.make_async_copy(
            result.at[h, side, i], outputs[i].at[0, :, columns(side, h)], local_sem.at[h, 4 + i]
        )

    def bias_copy(which):
        return pltpu.make_async_remote_copy(
            src_ref=bias.at[side],
            dst_ref=bias.at[which],
            send_sem=bias_sem.at[0],
            recv_sem=bias_sem.at[1],
            device_id={"mp": partner},
            device_id_type=MESH,
        )

    barrier = pltpu.get_barrier_semaphore()
    pl.semaphore_signal(barrier, inc=1, device_id={"mp": partner}, device_id_type=MESH)

    @pl.when(has_up)
    def _():
        pl.semaphore_signal(barrier, inc=1, device_id={"mp": up}, device_id_type=MESH)

    @pl.when(has_down)
    def _():
        pl.semaphore_signal(barrier, inc=1, device_id={"mp": down}, device_id_type=MESH)

    @pl.loop(0, HALF)
    def _(h):
        for i in range(4):
            keep(i, h).start()

    tile = 2 * pair - 2 + lax.broadcasted_iota(jnp.int32, (8, TILE), 0)
    present = tile == me
    listed_count = counts_ref[0, 0]
    near = (tile >= me - REACH) & (tile <= me + REACH)
    for place_at in range(MAXN):
        wanted = neighbours_ref[0, 0, place_at]
        wanted = jnp.where(place_at < listed_count, wanted, -1000)
        present = present | (near & (tile == wanted))
    bias[side] = jnp.where(present, 0.0, -jnp.inf).astype(jnp.float32)

    pl.semaphore_wait(barrier, 1 + has_up.astype(jnp.int32) + has_down.astype(jnp.int32))

    bias_copy(side).start()

    @pl.loop(0, HALF)
    def _(h):
        give(0, h).start()
        give(1, h).start()

        @pl.when(has_up)
        def _():
            own_up(0, h).start()
            own_up(1, h).start()

        @pl.when(has_down)
        def _():
            own_down(0, h).start()
            own_down(1, h).start()

        give(2, h).start()
        give(3, h).start()


    def clear(ref, slot):
        @pl.loop(0, HALF)
        def _(h):
            ref[h, slot] = jnp.zeros((2, 2, TILE, HEAD_DIM), jnp.bfloat16)

    @pl.when(jnp.logical_not(has_down))
    def _():
        clear(kv, 0)
        clear(share_in, 0)

    @pl.when(jnp.logical_not(has_up))
    def _():
        clear(kv, 2)
        clear(share_in, 1)

    def forward(h):
        take(0, h).wait_recv()
        take(1, h).wait_recv()

        @pl.when(has_up)
        def _():
            pass_up(h).start()

        @pl.when(has_down)
        def _():
            pass_down(h).start()

    def gather(h):
        for i in range(4):
            keep(i, h).wait()
        take(2, h).wait_recv()
        take(3, h).wait_recv()

        @pl.when(has_down)
        def _():
            own_up(0, h).wait_recv()
            own_up(1, h).wait_recv()
            pass_up(h).wait_recv()

        @pl.when(has_up)
        def _():
            own_down(0, h).wait_recv()
            own_down(1, h).wait_recv()
            pass_down(h).wait_recv()

    def attend(h):
        query = qg[h, :, 0].reshape(2 * TILE, HEAD_DIM)
        grad = qg[h, :, 1].reshape(2 * TILE, HEAD_DIM)
        keys = [kv[h, s // 2, s % 2, 0] for s in range(SLOTS)]
        values = [kv[h, s // 2, s % 2, 1] for s in range(SLOTS)]
        scores = []
        for s in range(SLOTS):
            row = jnp.concatenate([bias[0, s : s + 1, :], bias[1, s : s + 1, :]], axis=1)
            scores.append(nt(keys[s], query) * INV_ROOT + row)
        top = scores[0]
        for s in range(1, SLOTS):
            top = jnp.maximum(top, scores[s])
        top = jnp.max(top, axis=0, keepdims=True)
        powers = [jnp.exp(score - top) for score in scores]
        total = powers[0]
        for s in range(1, SLOTS):
            total = total + powers[s]
        scale = 1.0 / jnp.sum(total, axis=0, keepdims=True)
        weights = [power * scale for power in powers]
        low = [weight.astype(jnp.bfloat16) for weight in weights]
        prob = [nt(values[s], grad) for s in range(SLOTS)]
        delta = low[0].astype(jnp.float32) * prob[0]
        for s in range(1, SLOTS):
            delta = delta + low[s].astype(jnp.float32) * prob[s]
        delta = jnp.sum(delta, axis=0, keepdims=True)
        dscore = [
            (weights[s] * (prob[s] - delta) * INV_ROOT).astype(jnp.bfloat16) for s in range(SLOTS)
        ]
        mixture = jnp.zeros((HEAD_DIM, 2 * TILE), jnp.float32)
        grad_query = jnp.zeros((HEAD_DIM, 2 * TILE), jnp.float32)
        for s in range(SLOTS):
            key_share = nn(dscore[s], query)
            value_share = nn(low[s], grad)
            if s // 2 == 1:
                own[h, s % 2, 0] = key_share
                own[h, s % 2, 1] = value_share
            else:
                share_out[h, s // 4, s % 2, 0] = key_share.astype(jnp.bfloat16)
                share_out[h, s // 4, s % 2, 1] = value_share.astype(jnp.bfloat16)
            mixture = mixture + nn(values[s].T, low[s])
            grad_query = grad_query + nn(keys[s].T, dscore[s])
        mixture = mixture.T.astype(jnp.bfloat16)
        grad_query = grad_query.T.astype(jnp.bfloat16)
        for which in range(2):
            rows = slice(which * TILE, (which + 1) * TILE)
            result[h, which, 0] = mixture[rows]
            result[h, which, 1] = grad_query[rows]

    def finish(h):
        @pl.when(has_down)
        def _():
            share_up(h).wait_recv()

        @pl.when(has_up)
        def _():
            share_down(h).wait_recv()

        total = (
            own[h]
            + share_in[h, 0].astype(jnp.float32)
            + share_in[h, 1].astype(jnp.float32)
        ).astype(jnp.bfloat16)
        for which in range(2):
            result[h, which, 2] = total[which, 0]
            result[h, which, 3] = total[which, 1]
        for i in range(2, 4):
            hand_back(i, h).start()
            write(i, h).start()

    for h in range(AHEAD):
        forward(h)
    bias_copy(other).wait_recv()

    @pl.loop(0, HALF)
    def _(h):
        @pl.when(h + AHEAD < HALF)
        def _():
            forward(h + AHEAD)

        gather(h)
        attend(h)

        @pl.when(has_up)
        def _():
            share_up(h).start()

        @pl.when(has_down)
        def _():
            share_down(h).start()

        for i in range(2):
            hand_back(i, h).start()
            write(i, h).start()

        @pl.when(h >= BEHIND)
        def _():
            finish(h - BEHIND)

    for h in range(HALF - BEHIND, HALF):
        finish(h)

    bias_copy(side).wait_send()

    @pl.loop(0, HALF)
    def _(h):
        for i in range(4):
            give(i, h).wait_send()
            write(i, h).wait()
            take_back(i, h).wait_recv()
            hand_back(i, h).wait_send()

        @pl.when(has_up)
        def _():
            own_up(0, h).wait_send()
            own_up(1, h).wait_send()
            pass_up(h).wait_send()
            share_up(h).wait_send()

        @pl.when(has_down)
        def _():
            own_down(0, h).wait_send()
            own_down(1, h).wait_send()
            pass_down(h).wait_send()
            share_down(h).wait_send()


def local(peers, queries, keys, values, grad_out, neighbours, counts):
    rows, tokens, features = queries.shape
    anywhere = pl.BlockSpec(memory_space=pl.ANY)
    scalars = pl.BlockSpec(memory_space=pltpu.SMEM)
    out = jax.ShapeDtypeStruct((rows, tokens, features), jnp.bfloat16)
    return tuple(
        pl.pallas_call(
            functools.partial(kernel, peers),
            out_shape=(out, out, out, out),
            in_specs=[scalars, scalars, anywhere, anywhere, anywhere, anywhere],
            out_specs=(anywhere, anywhere, anywhere, anywhere),
            scratch_shapes=[
                pltpu.VMEM((HALF, 3, 2, 2, TILE, HEAD_DIM), jnp.bfloat16),
                pltpu.VMEM((HALF, 2, 2, TILE, HEAD_DIM), jnp.bfloat16),
                pltpu.VMEM((HALF, 2, 2, 2, TILE, HEAD_DIM), jnp.bfloat16),
                pltpu.VMEM((HALF, 2, 2, 2, TILE, HEAD_DIM), jnp.bfloat16),
                pltpu.VMEM((HALF, 2, 4, TILE, HEAD_DIM), jnp.bfloat16),
                pltpu.VMEM((HALF, 2, 2, TILE, HEAD_DIM), jnp.float32),
                pltpu.VMEM((2, 8, TILE), jnp.float32),
                pltpu.SemaphoreType.DMA((HALF, 16)),
                pltpu.SemaphoreType.DMA((HALF, 16)),
                pltpu.SemaphoreType.DMA((HALF, 8)),
                pltpu.SemaphoreType.DMA((2,)),
            ],
            compiler_params=pltpu.CompilerParams(
                collective_id=0, has_side_effects=True, vmem_limit_bytes=40 * 1024 * 1024
            ),
            cost_estimate=pl.CostEstimate(
                flops=2_500_000_000, bytes_accessed=4_194_304, transcendentals=1_600_000
            ),
        )(neighbours, counts, queries, keys, values, grad_out)
    )


def solution(mesh):
    spec = P(("groups", "dp"), "mp", None)
    return jax.shard_map(
        functools.partial(local, mesh.shape["mp"]),
        mesh=mesh,
        in_specs=(spec, spec, spec, spec, spec, P(("groups", "dp"), "mp")),
        out_specs=(spec, spec, spec, spec),
        check_vma=False,
    )
```

```python
import functools

import jax
import jax.numpy as jnp
from jax import lax
from jax.experimental import pallas as pl
from jax.experimental.pallas import tpu as pltpu
from jax.sharding import PartitionSpec as P

HEADS = 16
HEAD_DIM = 128
TILE = 128
REACH = 2
MAXN = 4
HALF = HEADS // 2
SLOTS = 6
AHEAD = 2
BEHIND = 2
INV_ROOT = HEAD_DIM ** (-0.5)
MESH = pl.DeviceIdType.MESH


def nt(a, b):
    return lax.dot_general(a, b, (((1,), (1,)), ((), ())), preferred_element_type=jnp.float32)


def nn(a, b):
    return jnp.dot(a, b, preferred_element_type=jnp.float32)


def kernel(
    peers,
    neighbours_ref, counts_ref, q_ref, k_ref, v_ref, g_ref,
    att_ref, gq_ref, gk_ref, gv_ref,
    kv, qg, share_out, share_in, result, own, bias,
    send_sem, recv_sem, local_sem, bias_sem,
):
    me = lax.axis_index("mp")
    side = lax.rem(me, 2)
    other = 1 - side
    partner = me + 1 - 2 * side
    pair = lax.div(me, 2)
    has_up = me + 2 < peers
    has_down = me >= 2
    up = me + 2
    down = me - 2
    width = HALF * HEAD_DIM

    def columns(half, h):
        return pl.ds(pl.multiple_of(half * width + h * HEAD_DIM, HEAD_DIM), HEAD_DIM)

    def remote(src, dst, stream, h, target):
        return pltpu.make_async_remote_copy(
            src_ref=src,
            dst_ref=dst,
            send_sem=send_sem.at[h, stream],
            recv_sem=recv_sem.at[h, stream],
            device_id={"mp": target},
            device_id_type=MESH,
        )

    inputs = (k_ref, v_ref, q_ref, g_ref)
    outputs = (att_ref, gq_ref, gk_ref, gv_ref)

    def place(i, h, which):
        return kv.at[h, 1, which, i] if i < 2 else qg.at[h, which, i - 2]

    def give(i, h):
        return remote(
            inputs[i].at[0, :, columns(other, h)], place(i, h, side), i, h, partner
        )

    def take(i, h):
        return remote(
            inputs[i].at[0, :, columns(other, h)], place(i, h, other), i, h, partner
        )

    def keep(i, h):
        return pltpu.make_async_copy(
            inputs[i].at[0, :, columns(side, h)], place(i, h, side), local_sem.at[h, i]
        )

    def own_up(i, h):
        return remote(inputs[i].at[0, :, columns(side, h)], kv.at[h, 0, side, i], 4 + i, h, up)

    def own_down(i, h):
        return remote(inputs[i].at[0, :, columns(side, h)], kv.at[h, 2, side, i], 6 + i, h, down)

    def pass_up(h):
        return remote(kv.at[h, 1, other], kv.at[h, 0, other], 8, h, up)

    def pass_down(h):
        return remote(kv.at[h, 1, other], kv.at[h, 2, other], 9, h, down)

    def share_up(h):
        return remote(share_out.at[h, 1], share_in.at[h, 0], 10, h, up)

    def share_down(h):
        return remote(share_out.at[h, 0], share_in.at[h, 1], 11, h, down)

    def hand_back(i, h):
        return remote(
            result.at[h, other, i], outputs[i].at[0, :, columns(side, h)], 12 + i, h, partner
        )

    def take_back(i, h):
        return remote(
            result.at[h, other, i], outputs[i].at[0, :, columns(other, h)], 12 + i, h, partner
        )

    def write(i, h):
        return pltpu.make_async_copy(
            result.at[h, side, i], outputs[i].at[0, :, columns(side, h)], local_sem.at[h, 4 + i]
        )

    def bias_copy(which):
        return pltpu.make_async_remote_copy(
            src_ref=bias.at[side],
            dst_ref=bias.at[which],
            send_sem=bias_sem.at[0],
            recv_sem=bias_sem.at[1],
            device_id={"mp": partner},
            device_id_type=MESH,
        )

    barrier = pltpu.get_barrier_semaphore()
    pl.semaphore_signal(barrier, inc=1, device_id={"mp": partner}, device_id_type=MESH)

    @pl.when(has_up)
    def _():
        pl.semaphore_signal(barrier, inc=1, device_id={"mp": up}, device_id_type=MESH)

    @pl.when(has_down)
    def _():
        pl.semaphore_signal(barrier, inc=1, device_id={"mp": down}, device_id_type=MESH)

    @pl.loop(0, HALF)
    def _(h):
        for i in range(4):
            keep(i, h).start()

    tile = 2 * pair - 2 + lax.broadcasted_iota(jnp.int32, (8, TILE), 0)
    present = tile == me
    listed_count = counts_ref[0, 0]
    near = (tile >= me - REACH) & (tile <= me + REACH)
    for place_at in range(MAXN):
        wanted = neighbours_ref[0, 0, place_at]
        wanted = jnp.where(place_at < listed_count, wanted, -1000)
        present = present | (near & (tile == wanted))
    bias[side] = jnp.where(present, 0.0, -jnp.inf).astype(jnp.float32)

    pl.semaphore_wait(barrier, 1 + has_up.astype(jnp.int32) + has_down.astype(jnp.int32))

    bias_copy(side).start()

    @pl.loop(0, HALF)
    def _(h):
        give(0, h).start()
        give(1, h).start()

        @pl.when(has_up)
        def _():
            own_up(0, h).start()
            own_up(1, h).start()

        @pl.when(has_down)
        def _():
            own_down(0, h).start()
            own_down(1, h).start()

        give(2, h).start()
        give(3, h).start()


    def clear(ref, slot):
        @pl.loop(0, HALF)
        def _(h):
            ref[h, slot] = jnp.zeros((2, 2, TILE, HEAD_DIM), jnp.bfloat16)

    @pl.when(jnp.logical_not(has_down))
    def _():
        clear(kv, 0)
        clear(share_in, 0)

    @pl.when(jnp.logical_not(has_up))
    def _():
        clear(kv, 2)
        clear(share_in, 1)

    def forward(h):
        take(0, h).wait_recv()
        take(1, h).wait_recv()

        @pl.when(has_up)
        def _():
            pass_up(h).start()

        @pl.when(has_down)
        def _():
            pass_down(h).start()

    def gather(h):
        for i in range(4):
            keep(i, h).wait()
        take(2, h).wait_recv()
        take(3, h).wait_recv()

        @pl.when(has_down)
        def _():
            own_up(0, h).wait_recv()
            own_up(1, h).wait_recv()
            pass_up(h).wait_recv()

        @pl.when(has_up)
        def _():
            own_down(0, h).wait_recv()
            own_down(1, h).wait_recv()
            pass_down(h).wait_recv()

    def attend(h):
        query = qg[h, :, 0].reshape(2 * TILE, HEAD_DIM)
        grad = qg[h, :, 1].reshape(2 * TILE, HEAD_DIM)
        keys = [kv[h, s // 2, s % 2, 0] for s in range(SLOTS)]
        values = [kv[h, s // 2, s % 2, 1] for s in range(SLOTS)]
        scores = []
        for s in range(SLOTS):
            row = jnp.concatenate([bias[0, s : s + 1, :], bias[1, s : s + 1, :]], axis=1)
            scores.append(nt(keys[s], query) * INV_ROOT + row)
        top = scores[0]
        for s in range(1, SLOTS):
            top = jnp.maximum(top, scores[s])
        top = jnp.max(top, axis=0, keepdims=True)
        powers = [jnp.exp(score - top) for score in scores]
        total = powers[0]
        for s in range(1, SLOTS):
            total = total + powers[s]
        scale = 1.0 / jnp.sum(total, axis=0, keepdims=True)
        weights = [power * scale for power in powers]
        low = [weight.astype(jnp.bfloat16) for weight in weights]
        prob = [nt(values[s], grad) for s in range(SLOTS)]
        delta = low[0].astype(jnp.float32) * prob[0]
        for s in range(1, SLOTS):
            delta = delta + low[s].astype(jnp.float32) * prob[s]
        delta = jnp.sum(delta, axis=0, keepdims=True)
        dscore = [
            (weights[s] * (prob[s] - delta) * INV_ROOT).astype(jnp.bfloat16) for s in range(SLOTS)
        ]
        mixture = jnp.zeros((HEAD_DIM, 2 * TILE), jnp.float32)
        grad_query = jnp.zeros((HEAD_DIM, 2 * TILE), jnp.float32)
        for s in range(SLOTS):
            key_share = nn(dscore[s], query)
            value_share = nn(low[s], grad)
            if s // 2 == 1:
                own[h, s % 2, 0] = key_share
                own[h, s % 2, 1] = value_share
            else:
                share_out[h, s // 4, s % 2, 0] = key_share.astype(jnp.bfloat16)
                share_out[h, s // 4, s % 2, 1] = value_share.astype(jnp.bfloat16)
            mixture = mixture + nn(values[s].T, low[s])
            grad_query = grad_query + nn(keys[s].T, dscore[s])
        mixture = mixture.T.astype(jnp.bfloat16)
        grad_query = grad_query.T.astype(jnp.bfloat16)
        for which in range(2):
            rows = slice(which * TILE, (which + 1) * TILE)
            result[h, which, 0] = mixture[rows]
            result[h, which, 1] = grad_query[rows]

    def finish(h):
        @pl.when(has_down)
        def _():
            share_up(h).wait_recv()

        @pl.when(has_up)
        def _():
            share_down(h).wait_recv()

        total = (
            own[h]
            + share_in[h, 0].astype(jnp.float32)
            + share_in[h, 1].astype(jnp.float32)
        ).astype(jnp.bfloat16)
        for which in range(2):
            result[h, which, 2] = total[which, 0]
            result[h, which, 3] = total[which, 1]
        for i in range(2, 4):
            hand_back(i, h).start()
            write(i, h).start()

    for h in range(AHEAD):
        forward(h)
    bias_copy(other).wait_recv()

    @pl.loop(0, HALF)
    def _(h):
        @pl.when(h + AHEAD < HALF)
        def _():
            forward(h + AHEAD)

        gather(h)
        attend(h)

        @pl.when(has_up)
        def _():
            share_up(h).start()

        @pl.when(has_down)
        def _():
            share_down(h).start()

        for i in range(2):
            hand_back(i, h).start()
            write(i, h).start()

        @pl.when(h >= BEHIND)
        def _():
            finish(h - BEHIND)

    for h in range(HALF - BEHIND, HALF):
        finish(h)

    bias_copy(side).wait_send()

    @pl.loop(0, HALF)
    def _(h):
        for i in range(4):
            give(i, h).wait_send()
            write(i, h).wait()
            take_back(i, h).wait_recv()
            hand_back(i, h).wait_send()

        @pl.when(has_up)
        def _():
            own_up(0, h).wait_send()
            own_up(1, h).wait_send()
            pass_up(h).wait_send()
            share_up(h).wait_send()

        @pl.when(has_down)
        def _():
            own_down(0, h).wait_send()
            own_down(1, h).wait_send()
            pass_down(h).wait_send()
            share_down(h).wait_send()


def settle(*refs):
    sources, targets, staged, sem = refs[:4], refs[4:8], refs[8], refs[9]
    reads = [pltpu.make_async_copy(sources[i], staged.at[i], sem.at[0, i]) for i in range(4)]
    writes = [pltpu.make_async_copy(staged.at[i], targets[i], sem.at[1, i]) for i in range(4)]
    for read in reads:
        read.start()
    for read, write in zip(reads, writes):
        read.wait()
        write.start()
    for write in writes:
        write.wait()


def local(peers, queries, keys, values, grad_out, neighbours, counts):
    rows, tokens, features = queries.shape
    anywhere = pl.BlockSpec(memory_space=pl.ANY)
    scalars = pl.BlockSpec(memory_space=pltpu.SMEM)
    out = jax.ShapeDtypeStruct((rows, tokens, features), jnp.bfloat16)
    packed = pl.pallas_call(
            functools.partial(kernel, peers),
            out_shape=(out, out, out, out),
            in_specs=[scalars, scalars, anywhere, anywhere, anywhere, anywhere],
            out_specs=(anywhere, anywhere, anywhere, anywhere),
            scratch_shapes=[
                pltpu.VMEM((HALF, 3, 2, 2, TILE, HEAD_DIM), jnp.bfloat16),
                pltpu.VMEM((HALF, 2, 2, TILE, HEAD_DIM), jnp.bfloat16),
                pltpu.VMEM((HALF, 2, 2, 2, TILE, HEAD_DIM), jnp.bfloat16),
                pltpu.VMEM((HALF, 2, 2, 2, TILE, HEAD_DIM), jnp.bfloat16),
                pltpu.VMEM((HALF, 2, 4, TILE, HEAD_DIM), jnp.bfloat16),
                pltpu.VMEM((HALF, 2, 2, TILE, HEAD_DIM), jnp.float32),
                pltpu.VMEM((2, 8, TILE), jnp.float32),
                pltpu.SemaphoreType.DMA((HALF, 16)),
                pltpu.SemaphoreType.DMA((HALF, 16)),
                pltpu.SemaphoreType.DMA((HALF, 8)),
                pltpu.SemaphoreType.DMA((2,)),
            ],
            compiler_params=pltpu.CompilerParams(
                collective_id=0, has_side_effects=True, vmem_limit_bytes=60 * 1024 * 1024
            ),
            cost_estimate=pl.CostEstimate(
                flops=2_500_000_000, bytes_accessed=4_194_304, transcendentals=1_600_000
            ),
        )(neighbours, counts, queries, keys, values, grad_out)
    return tuple(
        pl.pallas_call(
            settle,
            out_shape=(out, out, out, out),
            in_specs=[anywhere] * 4,
            out_specs=(anywhere,) * 4,
            scratch_shapes=[
                pltpu.VMEM((4, rows, tokens, features), jnp.bfloat16),
                pltpu.SemaphoreType.DMA((2, 4)),
            ],
        )(*packed)
    )


def solution(mesh):
    spec = P(("groups", "dp"), "mp", None)
    return jax.shard_map(
        functools.partial(local, mesh.shape["mp"]),
        mesh=mesh,
        in_specs=(spec, spec, spec, spec, spec, P(("groups", "dp"), "mp")),
        out_specs=(spec, spec, spec, spec),
        check_vma=False,
    )
```

```python
import functools

import jax
import jax.numpy as jnp
from jax import lax
from jax.experimental import pallas as pl
from jax.experimental.pallas import tpu as pltpu
from jax.sharding import PartitionSpec as P

HEADS = 16
HEAD_DIM = 128
TILE = 128
REACH = 2
MAXN = 4
HALF = HEADS // 2
SLOTS = 6
AHEAD = 2
BEHIND = 2
LATE = 4
INV_ROOT = HEAD_DIM ** (-0.5)
MESH = pl.DeviceIdType.MESH


def nt(a, b):
    return lax.dot_general(a, b, (((1,), (1,)), ((), ())), preferred_element_type=jnp.float32)


def nn(a, b):
    return jnp.dot(a, b, preferred_element_type=jnp.float32)


def kernel(
    peers,
    near_ref, count_ref, q_ref, k_ref, v_ref, g_ref,
    att_ref, gq_ref, gk_ref, gv_ref,
    kv, qg, share_out, share_in, result, own, bias,
    neighbours_ref, counts_ref, send_sem, recv_sem, local_sem, bias_sem, list_sem,
):
    me = lax.axis_index("mp")
    side = lax.rem(me, 2)
    other = 1 - side
    partner = me + 1 - 2 * side
    pair = lax.div(me, 2)
    has_up = me + 2 < peers
    has_down = me >= 2
    up = me + 2
    down = me - 2
    width = HALF * HEAD_DIM

    def columns(half, h):
        return pl.ds(pl.multiple_of(half * width + h * HEAD_DIM, HEAD_DIM), HEAD_DIM)

    def remote(src, dst, stream, h, target):
        return pltpu.make_async_remote_copy(
            src_ref=src,
            dst_ref=dst,
            send_sem=send_sem.at[h, stream],
            recv_sem=recv_sem.at[h, stream],
            device_id={"mp": target},
            device_id_type=MESH,
        )

    inputs = (k_ref, v_ref, q_ref, g_ref)
    outputs = (att_ref, gq_ref, gk_ref, gv_ref)

    def place(i, h, which):
        return kv.at[h, 1, which, i] if i < 2 else qg.at[h, which, i - 2]

    def give(i, h):
        return remote(
            inputs[i].at[0, :, columns(other, h)], place(i, h, side), i, h, partner
        )

    def take(i, h):
        return remote(
            inputs[i].at[0, :, columns(other, h)], place(i, h, other), i, h, partner
        )

    def keep(i, h):
        return pltpu.make_async_copy(
            inputs[i].at[0, :, columns(side, h)], place(i, h, side), local_sem.at[h, i]
        )

    def own_up(i, h):
        return remote(inputs[i].at[0, :, columns(side, h)], kv.at[h, 0, side, i], 4 + i, h, up)

    def own_down(i, h):
        return remote(inputs[i].at[0, :, columns(side, h)], kv.at[h, 2, side, i], 6 + i, h, down)

    def pass_up(h):
        return remote(kv.at[h, 1, other], kv.at[h, 0, other], 8, h, up)

    def pass_down(h):
        return remote(kv.at[h, 1, other], kv.at[h, 2, other], 9, h, down)

    def share_up(h):
        return remote(share_out.at[h, 1], share_in.at[h, 0], 10, h, up)

    def share_down(h):
        return remote(share_out.at[h, 0], share_in.at[h, 1], 11, h, down)

    def hand_back(i, h):
        return remote(
            result.at[h, other, i], outputs[i].at[0, :, columns(side, h)], 12 + i, h, partner
        )

    def take_back(i, h):
        return remote(
            result.at[h, other, i], outputs[i].at[0, :, columns(other, h)], 12 + i, h, partner
        )

    def write(i, h):
        return pltpu.make_async_copy(
            result.at[h, side, i], outputs[i].at[0, :, columns(side, h)], local_sem.at[h, 4 + i]
        )

    def bias_copy(which):
        return pltpu.make_async_remote_copy(
            src_ref=bias.at[side],
            dst_ref=bias.at[which],
            send_sem=bias_sem.at[0],
            recv_sem=bias_sem.at[1],
            device_id={"mp": partner},
            device_id_type=MESH,
        )

    barrier = pltpu.get_barrier_semaphore()
    pl.semaphore_signal(barrier, inc=1, device_id={"mp": partner}, device_id_type=MESH)

    @pl.when(has_up)
    def _():
        pl.semaphore_signal(barrier, inc=1, device_id={"mp": up}, device_id_type=MESH)

    @pl.when(has_down)
    def _():
        pl.semaphore_signal(barrier, inc=1, device_id={"mp": down}, device_id_type=MESH)

    lists = (
        pltpu.make_async_copy(near_ref, neighbours_ref, list_sem.at[0]),
        pltpu.make_async_copy(count_ref, counts_ref, list_sem.at[1]),
    )
    for copy in lists:
        copy.start()

    @pl.loop(0, HALF)
    def _(h):
        for i in range(4):
            keep(i, h).start()

    for copy in lists:
        copy.wait()
    tile = 2 * pair - 2 + lax.broadcasted_iota(jnp.int32, (8, TILE), 0)
    present = tile == me
    listed_count = counts_ref[0, 0]
    near = (tile >= me - REACH) & (tile <= me + REACH)
    for place_at in range(MAXN):
        wanted = neighbours_ref[0, 0, place_at]
        wanted = jnp.where(place_at < listed_count, wanted, -1000)
        present = present | (near & (tile == wanted))
    bias[side] = jnp.where(present, 0.0, -jnp.inf).astype(jnp.float32)

    pl.semaphore_wait(barrier, 1 + has_up.astype(jnp.int32) + has_down.astype(jnp.int32))

    bias_copy(side).start()

    @pl.loop(0, HALF)
    def _(h):
        give(0, h).start()
        give(1, h).start()

        @pl.when(has_up)
        def _():
            own_up(0, h).start()
            own_up(1, h).start()

        @pl.when(has_down)
        def _():
            own_down(0, h).start()
            own_down(1, h).start()

        give(2, h).start()
        give(3, h).start()


    def clear(ref, slot):
        @pl.loop(0, HALF)
        def _(h):
            ref[h, slot] = jnp.zeros((2, 2, TILE, HEAD_DIM), jnp.bfloat16)

    @pl.when(jnp.logical_not(has_down))
    def _():
        clear(kv, 0)
        clear(share_in, 0)

    @pl.when(jnp.logical_not(has_up))
    def _():
        clear(kv, 2)
        clear(share_in, 1)

    def forward(h):
        take(0, h).wait_recv()
        take(1, h).wait_recv()

        @pl.when(has_up)
        def _():
            pass_up(h).start()

        @pl.when(has_down)
        def _():
            pass_down(h).start()

    def gather(h):
        for i in range(4):
            keep(i, h).wait()
        take(2, h).wait_recv()
        take(3, h).wait_recv()

        @pl.when(has_down)
        def _():
            own_up(0, h).wait_recv()
            own_up(1, h).wait_recv()
            pass_up(h).wait_recv()

        @pl.when(has_up)
        def _():
            own_down(0, h).wait_recv()
            own_down(1, h).wait_recv()
            pass_down(h).wait_recv()

    def attend(h):
        query = qg[h, :, 0].reshape(2 * TILE, HEAD_DIM)
        grad = qg[h, :, 1].reshape(2 * TILE, HEAD_DIM)
        keys = [kv[h, s // 2, s % 2, 0] for s in range(SLOTS)]
        values = [kv[h, s // 2, s % 2, 1] for s in range(SLOTS)]
        scores = []
        for s in range(SLOTS):
            row = jnp.concatenate([bias[0, s : s + 1, :], bias[1, s : s + 1, :]], axis=1)
            scores.append(nt(keys[s], query) * INV_ROOT + row)
        top = scores[0]
        for s in range(1, SLOTS):
            top = jnp.maximum(top, scores[s])
        top = jnp.max(top, axis=0, keepdims=True)
        powers = [jnp.exp(score - top) for score in scores]
        total = powers[0]
        for s in range(1, SLOTS):
            total = total + powers[s]
        scale = 1.0 / jnp.sum(total, axis=0, keepdims=True)
        weights = [power * scale for power in powers]
        low = [weight.astype(jnp.bfloat16) for weight in weights]
        prob = [nt(values[s], grad) for s in range(SLOTS)]
        delta = low[0].astype(jnp.float32) * prob[0]
        for s in range(1, SLOTS):
            delta = delta + low[s].astype(jnp.float32) * prob[s]
        delta = jnp.sum(delta, axis=0, keepdims=True)
        dscore = [
            (weights[s] * (prob[s] - delta) * INV_ROOT).astype(jnp.bfloat16) for s in range(SLOTS)
        ]
        mixture = jnp.zeros((HEAD_DIM, 2 * TILE), jnp.float32)
        grad_query = jnp.zeros((HEAD_DIM, 2 * TILE), jnp.float32)
        for s in range(SLOTS):
            key_share = nn(dscore[s], query)
            value_share = nn(low[s], grad)
            if s // 2 == 1:
                own[h, s % 2, 0] = key_share
                own[h, s % 2, 1] = value_share
            else:
                share_out[h, s // 4, s % 2, 0] = key_share.astype(jnp.bfloat16)
                share_out[h, s // 4, s % 2, 1] = value_share.astype(jnp.bfloat16)
            mixture = mixture + nn(values[s].T, low[s])
            grad_query = grad_query + nn(keys[s].T, dscore[s])
        mixture = mixture.T.astype(jnp.bfloat16)
        grad_query = grad_query.T.astype(jnp.bfloat16)
        for which in range(2):
            rows = slice(which * TILE, (which + 1) * TILE)
            result[h, which, 0] = mixture[rows]
            result[h, which, 1] = grad_query[rows]

    def finish(h):
        @pl.when(has_down)
        def _():
            share_up(h).wait_recv()

        @pl.when(has_up)
        def _():
            share_down(h).wait_recv()

        total = (
            own[h]
            + share_in[h, 0].astype(jnp.float32)
            + share_in[h, 1].astype(jnp.float32)
        ).astype(jnp.bfloat16)
        for which in range(2):
            result[h, which, 2] = total[which, 0]
            result[h, which, 3] = total[which, 1]
        for i in range(2, 4):
            hand_back(i, h).start()
            write(i, h).start()

    for h in range(AHEAD):
        forward(h)
    bias_copy(other).wait_recv()

    @pl.loop(0, HALF)
    def _(h):
        @pl.when(h + AHEAD < HALF)
        def _():
            forward(h + AHEAD)

        gather(h)
        attend(h)

        @pl.when(has_up)
        def _():
            share_up(h).start()

        @pl.when(has_down)
        def _():
            share_down(h).start()

        for i in range(2):
            hand_back(i, h).start()
            write(i, h).start()

        @pl.when(h >= BEHIND)
        def _():
            finish(h - BEHIND)

    def drain_inputs(h):
        for i in range(4):
            give(i, h).wait_send()

        @pl.when(has_up)
        def _():
            own_up(0, h).wait_send()
            own_up(1, h).wait_send()
            pass_up(h).wait_send()

        @pl.when(has_down)
        def _():
            own_down(0, h).wait_send()
            own_down(1, h).wait_send()
            pass_down(h).wait_send()

    def drain_outputs(h):
        for i in range(4):
            write(i, h).wait()
            hand_back(i, h).wait_send()
            take_back(i, h).wait_recv()

        @pl.when(has_up)
        def _():
            share_up(h).wait_send()

        @pl.when(has_down)
        def _():
            share_down(h).wait_send()

    bias_copy(side).wait_send()

    @pl.loop(0, HALF)
    def _(h):
        drain_inputs(h)

    @pl.loop(0, HALF - LATE)
    def _(h):
        drain_outputs(h)

    for h in range(HALF - BEHIND, HALF):
        finish(h)

    @pl.loop(HALF - LATE, HALF)
    def _(h):
        drain_outputs(h)


def settle(a_ref, b_ref, c_ref, d_ref, p_ref, q_ref, r_ref, s_ref, sem):
    pairs = zip((a_ref, b_ref, c_ref, d_ref), (p_ref, q_ref, r_ref, s_ref))
    copies = [
        pltpu.make_async_copy(src, dst, sem.at[i]) for i, (src, dst) in enumerate(pairs)
    ]
    for copy in copies:
        copy.start()
    for copy in copies:
        copy.wait()


def local(peers, queries, keys, values, grad_out, neighbours, counts):
    rows, tokens, features = queries.shape
    anywhere = pl.BlockSpec(memory_space=pl.ANY)
    out = jax.ShapeDtypeStruct((rows, tokens, features), jnp.bfloat16)
    packed = pl.pallas_call(
            functools.partial(kernel, peers),
            out_shape=(pltpu.VMEM((rows, tokens, features), jnp.bfloat16),) * 4,
            in_specs=[anywhere, anywhere, anywhere, anywhere, anywhere, anywhere],
            out_specs=(pl.BlockSpec(memory_space=pltpu.VMEM),) * 4,
            scratch_shapes=[
                pltpu.VMEM((HALF, 3, 2, 2, TILE, HEAD_DIM), jnp.bfloat16),
                pltpu.VMEM((HALF, 2, 2, TILE, HEAD_DIM), jnp.bfloat16),
                pltpu.VMEM((HALF, 2, 2, 2, TILE, HEAD_DIM), jnp.bfloat16),
                pltpu.VMEM((HALF, 2, 2, 2, TILE, HEAD_DIM), jnp.bfloat16),
                pltpu.VMEM((HALF, 2, 4, TILE, HEAD_DIM), jnp.bfloat16),
                pltpu.VMEM((HALF, 2, 2, TILE, HEAD_DIM), jnp.float32),
                pltpu.VMEM((2, 8, TILE), jnp.float32),
                pltpu.SMEM(neighbours.shape, jnp.int32),
                pltpu.SMEM(counts.shape, jnp.int32),
                pltpu.SemaphoreType.DMA((HALF, 16)),
                pltpu.SemaphoreType.DMA((HALF, 16)),
                pltpu.SemaphoreType.DMA((HALF, 8)),
                pltpu.SemaphoreType.DMA((2,)),
                pltpu.SemaphoreType.DMA((2,)),
            ],
            compiler_params=pltpu.CompilerParams(
                collective_id=0, has_side_effects=True, vmem_limit_bytes=61 * 1024 * 1024
            ),
            cost_estimate=pl.CostEstimate(
                flops=2_500_000_000, bytes_accessed=4_194_304, transcendentals=1_600_000
            ),
        )(neighbours, counts, queries, keys, values, grad_out)
    return tuple(
        pl.pallas_call(
            settle,
            out_shape=(out, out, out, out),
            in_specs=[anywhere] * 4,
            out_specs=(anywhere,) * 4,
            scratch_shapes=[pltpu.SemaphoreType.DMA((4,))],
            compiler_params=pltpu.CompilerParams(vmem_limit_bytes=2 * 1024 * 1024),
        )(*packed)
    )


def solution(mesh):
    spec = P(("groups", "dp"), "mp", None)
    return jax.shard_map(
        functools.partial(local, mesh.shape["mp"]),
        mesh=mesh,
        in_specs=(spec, spec, spec, spec, spec, P(("groups", "dp"), "mp")),
        out_specs=(spec, spec, spec, spec),
        check_vma=False,
    )
```

```python
import functools

import jax
import jax.numpy as jnp
from jax import lax
from jax.experimental import pallas as pl
from jax.experimental.pallas import tpu as pltpu
from jax.sharding import PartitionSpec as P

HEADS = 16
HEAD_DIM = 128
TILE = 128
REACH = 2
MAXN = 4
HALF = HEADS // 2
SLOTS = 6
AHEAD = 3
BEHIND = 3
LATE = 5
INV_ROOT = HEAD_DIM ** (-0.5)
MESH = pl.DeviceIdType.MESH


def nt(a, b):
    return lax.dot_general(a, b, (((1,), (1,)), ((), ())), preferred_element_type=jnp.float32)


def nn(a, b):
    return jnp.dot(a, b, preferred_element_type=jnp.float32)


def kernel(
    peers,
    near_ref, count_ref, q_ref, k_ref, v_ref, g_ref,
    att_ref, gq_ref, gk_ref, gv_ref,
    kv, qg, share_out, share_in, result, own, bias,
    neighbours_ref, counts_ref, send_sem, recv_sem, local_sem, bias_sem, list_sem,
):
    me = lax.axis_index("mp")
    side = lax.rem(me, 2)
    other = 1 - side
    partner = me + 1 - 2 * side
    pair = lax.div(me, 2)
    has_up = me + 2 < peers
    has_down = me >= 2
    up = me + 2
    down = me - 2
    width = HALF * HEAD_DIM

    def columns(half, h):
        return pl.ds(pl.multiple_of(half * width + h * HEAD_DIM, HEAD_DIM), HEAD_DIM)

    def remote(src, dst, stream, h, target):
        return pltpu.make_async_remote_copy(
            src_ref=src,
            dst_ref=dst,
            send_sem=send_sem.at[h, stream],
            recv_sem=recv_sem.at[h, stream],
            device_id={"mp": target},
            device_id_type=MESH,
        )

    inputs = (k_ref, v_ref, q_ref, g_ref)
    outputs = (att_ref, gq_ref, gk_ref, gv_ref)

    def place(i, h, which):
        return kv.at[h, 1, which, i] if i < 2 else qg.at[h, which, i - 2]

    def give(i, h):
        return remote(
            inputs[i].at[0, :, columns(other, h)], place(i, h, side), i, h, partner
        )

    def take(i, h):
        return remote(
            inputs[i].at[0, :, columns(other, h)], place(i, h, other), i, h, partner
        )

    def keep(i, h):
        return pltpu.make_async_copy(
            inputs[i].at[0, :, columns(side, h)], place(i, h, side), local_sem.at[h, i]
        )

    def own_up(i, h):
        return remote(inputs[i].at[0, :, columns(side, h)], kv.at[h, 0, side, i], 4 + i, h, up)

    def own_down(i, h):
        return remote(inputs[i].at[0, :, columns(side, h)], kv.at[h, 2, side, i], 6 + i, h, down)

    def pass_up(h):
        return remote(kv.at[h, 1, other], kv.at[h, 0, other], 8, h, up)

    def pass_down(h):
        return remote(kv.at[h, 1, other], kv.at[h, 2, other], 9, h, down)

    def share_up(h):
        return remote(share_out.at[h, 1], share_in.at[h, 0], 10, h, up)

    def share_down(h):
        return remote(share_out.at[h, 0], share_in.at[h, 1], 11, h, down)

    def hand_back(i, h):
        return remote(
            result.at[h, other, i], outputs[i].at[0, :, columns(side, h)], 12 + i, h, partner
        )

    def take_back(i, h):
        return remote(
            result.at[h, other, i], outputs[i].at[0, :, columns(other, h)], 12 + i, h, partner
        )

    def write(i, h):
        return pltpu.make_async_copy(
            result.at[h, side, i], outputs[i].at[0, :, columns(side, h)], local_sem.at[h, 4 + i]
        )

    def bias_copy(which):
        return pltpu.make_async_remote_copy(
            src_ref=bias.at[side],
            dst_ref=bias.at[which],
            send_sem=bias_sem.at[0],
            recv_sem=bias_sem.at[1],
            device_id={"mp": partner},
            device_id_type=MESH,
        )

    barrier = pltpu.get_barrier_semaphore()
    pl.semaphore_signal(barrier, inc=1, device_id={"mp": partner}, device_id_type=MESH)

    @pl.when(has_up)
    def _():
        pl.semaphore_signal(barrier, inc=1, device_id={"mp": up}, device_id_type=MESH)

    @pl.when(has_down)
    def _():
        pl.semaphore_signal(barrier, inc=1, device_id={"mp": down}, device_id_type=MESH)

    lists = (
        pltpu.make_async_copy(near_ref, neighbours_ref, list_sem.at[0]),
        pltpu.make_async_copy(count_ref, counts_ref, list_sem.at[1]),
    )
    for copy in lists:
        copy.start()

    @pl.loop(0, HALF)
    def _(h):
        for i in range(4):
            keep(i, h).start()

    for copy in lists:
        copy.wait()
    tile = 2 * pair - 2 + lax.broadcasted_iota(jnp.int32, (8, TILE), 0)
    present = tile == me
    listed_count = counts_ref[0, 0]
    near = (tile >= me - REACH) & (tile <= me + REACH)
    for place_at in range(MAXN):
        wanted = neighbours_ref[0, 0, place_at]
        wanted = jnp.where(place_at < listed_count, wanted, -1000)
        present = present | (near & (tile == wanted))
    bias[side] = jnp.where(present, 0.0, -jnp.inf).astype(jnp.float32)

    pl.semaphore_wait(barrier, 1 + has_up.astype(jnp.int32) + has_down.astype(jnp.int32))

    bias_copy(side).start()

    @pl.loop(0, HALF)
    def _(h):
        give(0, h).start()
        give(1, h).start()

        @pl.when(has_up)
        def _():
            own_up(0, h).start()
            own_up(1, h).start()

        @pl.when(has_down)
        def _():
            own_down(0, h).start()
            own_down(1, h).start()

        give(2, h).start()
        give(3, h).start()


    def clear(ref, slot):
        @pl.loop(0, HALF)
        def _(h):
            ref[h, slot] = jnp.zeros((2, 2, TILE, HEAD_DIM), jnp.bfloat16)

    @pl.when(jnp.logical_not(has_down))
    def _():
        clear(kv, 0)
        clear(share_in, 0)

    @pl.when(jnp.logical_not(has_up))
    def _():
        clear(kv, 2)
        clear(share_in, 1)

    def forward(h):
        take(0, h).wait_recv()
        take(1, h).wait_recv()

        @pl.when(has_up)
        def _():
            pass_up(h).start()

        @pl.when(has_down)
        def _():
            pass_down(h).start()

    def gather(h):
        for i in range(4):
            keep(i, h).wait()
        take(2, h).wait_recv()
        take(3, h).wait_recv()

        @pl.when(has_down)
        def _():
            own_up(0, h).wait_recv()
            own_up(1, h).wait_recv()
            pass_up(h).wait_recv()

        @pl.when(has_up)
        def _():
            own_down(0, h).wait_recv()
            own_down(1, h).wait_recv()
            pass_down(h).wait_recv()

    def attend(h):
        query = qg[h, :, 0].reshape(2 * TILE, HEAD_DIM)
        grad = qg[h, :, 1].reshape(2 * TILE, HEAD_DIM)
        keys = [kv[h, s // 2, s % 2, 0] for s in range(SLOTS)]
        values = [kv[h, s // 2, s % 2, 1] for s in range(SLOTS)]
        scores = []
        for s in range(SLOTS):
            row = jnp.concatenate([bias[0, s : s + 1, :], bias[1, s : s + 1, :]], axis=1)
            scores.append(nt(keys[s], query) * INV_ROOT + row)
        top = scores[0]
        for s in range(1, SLOTS):
            top = jnp.maximum(top, scores[s])
        top = jnp.max(top, axis=0, keepdims=True)
        powers = [jnp.exp(score - top) for score in scores]
        total = powers[0]
        for s in range(1, SLOTS):
            total = total + powers[s]
        scale = 1.0 / jnp.sum(total, axis=0, keepdims=True)
        weights = [power * scale for power in powers]
        low = [weight.astype(jnp.bfloat16) for weight in weights]
        prob = [nt(values[s], grad) for s in range(SLOTS)]
        delta = low[0].astype(jnp.float32) * prob[0]
        for s in range(1, SLOTS):
            delta = delta + low[s].astype(jnp.float32) * prob[s]
        delta = jnp.sum(delta, axis=0, keepdims=True)
        dscore = [
            (weights[s] * (prob[s] - delta) * INV_ROOT).astype(jnp.bfloat16) for s in range(SLOTS)
        ]
        mixture = jnp.zeros((HEAD_DIM, 2 * TILE), jnp.float32)
        grad_query = jnp.zeros((HEAD_DIM, 2 * TILE), jnp.float32)
        for s in range(SLOTS):
            key_share = nn(dscore[s], query)
            value_share = nn(low[s], grad)
            if s // 2 == 1:
                own[h, s % 2, 0] = key_share
                own[h, s % 2, 1] = value_share
            else:
                share_out[h, s // 4, s % 2, 0] = key_share.astype(jnp.bfloat16)
                share_out[h, s // 4, s % 2, 1] = value_share.astype(jnp.bfloat16)
            mixture = mixture + nn(values[s].T, low[s])
            grad_query = grad_query + nn(keys[s].T, dscore[s])
        mixture = mixture.T.astype(jnp.bfloat16)
        grad_query = grad_query.T.astype(jnp.bfloat16)
        for which in range(2):
            rows = slice(which * TILE, (which + 1) * TILE)
            result[h, which, 0] = mixture[rows]
            result[h, which, 1] = grad_query[rows]

    def finish(h):
        @pl.when(has_down)
        def _():
            share_up(h).wait_recv()

        @pl.when(has_up)
        def _():
            share_down(h).wait_recv()

        total = (
            own[h]
            + share_in[h, 0].astype(jnp.float32)
            + share_in[h, 1].astype(jnp.float32)
        ).astype(jnp.bfloat16)
        for which in range(2):
            result[h, which, 2] = total[which, 0]
            result[h, which, 3] = total[which, 1]
        for i in range(2, 4):
            hand_back(i, h).start()
            write(i, h).start()

    for h in range(AHEAD):
        forward(h)
    bias_copy(other).wait_recv()

    @pl.loop(0, HALF)
    def _(h):
        @pl.when(h + AHEAD < HALF)
        def _():
            forward(h + AHEAD)

        gather(h)
        attend(h)

        @pl.when(has_up)
        def _():
            share_up(h).start()

        @pl.when(has_down)
        def _():
            share_down(h).start()

        for i in range(2):
            hand_back(i, h).start()
            write(i, h).start()

        @pl.when(h >= BEHIND)
        def _():
            finish(h - BEHIND)

    def drain_inputs(h):
        for i in range(4):
            give(i, h).wait_send()

        @pl.when(has_up)
        def _():
            own_up(0, h).wait_send()
            own_up(1, h).wait_send()
            pass_up(h).wait_send()

        @pl.when(has_down)
        def _():
            own_down(0, h).wait_send()
            own_down(1, h).wait_send()
            pass_down(h).wait_send()

    def drain_outputs(h):
        for i in range(4):
            write(i, h).wait()
            hand_back(i, h).wait_send()
            take_back(i, h).wait_recv()

        @pl.when(has_up)
        def _():
            share_up(h).wait_send()

        @pl.when(has_down)
        def _():
            share_down(h).wait_send()

    bias_copy(side).wait_send()

    @pl.loop(0, HALF)
    def _(h):
        drain_inputs(h)

    @pl.loop(0, HALF - LATE)
    def _(h):
        drain_outputs(h)

    for h in range(HALF - BEHIND, HALF):
        finish(h)

    @pl.loop(HALF - LATE, HALF)
    def _(h):
        drain_outputs(h)


def settle(a_ref, b_ref, c_ref, d_ref, p_ref, q_ref, r_ref, s_ref, sem):
    pairs = zip((a_ref, b_ref, c_ref, d_ref), (p_ref, q_ref, r_ref, s_ref))
    copies = [
        pltpu.make_async_copy(src, dst, sem.at[i]) for i, (src, dst) in enumerate(pairs)
    ]
    for copy in copies:
        copy.start()
    for copy in copies:
        copy.wait()


def local(peers, queries, keys, values, grad_out, neighbours, counts):
    rows, tokens, features = queries.shape
    anywhere = pl.BlockSpec(memory_space=pl.ANY)
    out = jax.ShapeDtypeStruct((rows, tokens, features), jnp.bfloat16)
    packed = pl.pallas_call(
            functools.partial(kernel, peers),
            out_shape=(pltpu.VMEM((rows, tokens, features), jnp.bfloat16),) * 4,
            in_specs=[anywhere, anywhere, anywhere, anywhere, anywhere, anywhere],
            out_specs=(pl.BlockSpec(memory_space=pltpu.VMEM),) * 4,
            scratch_shapes=[
                pltpu.VMEM((HALF, 3, 2, 2, TILE, HEAD_DIM), jnp.bfloat16),
                pltpu.VMEM((HALF, 2, 2, TILE, HEAD_DIM), jnp.bfloat16),
                pltpu.VMEM((HALF, 2, 2, 2, TILE, HEAD_DIM), jnp.bfloat16),
                pltpu.VMEM((HALF, 2, 2, 2, TILE, HEAD_DIM), jnp.bfloat16),
                pltpu.VMEM((HALF, 2, 4, TILE, HEAD_DIM), jnp.bfloat16),
                pltpu.VMEM((HALF, 2, 2, TILE, HEAD_DIM), jnp.float32),
                pltpu.VMEM((2, 8, TILE), jnp.float32),
                pltpu.SMEM(neighbours.shape, jnp.int32),
                pltpu.SMEM(counts.shape, jnp.int32),
                pltpu.SemaphoreType.DMA((HALF, 16)),
                pltpu.SemaphoreType.DMA((HALF, 16)),
                pltpu.SemaphoreType.DMA((HALF, 8)),
                pltpu.SemaphoreType.DMA((2,)),
                pltpu.SemaphoreType.DMA((2,)),
            ],
            compiler_params=pltpu.CompilerParams(
                collective_id=0, has_side_effects=True, vmem_limit_bytes=61 * 1024 * 1024
            ),
            cost_estimate=pl.CostEstimate(
                flops=2_500_000_000, bytes_accessed=4_194_304, transcendentals=1_600_000
            ),
        )(neighbours, counts, queries, keys, values, grad_out)
    return tuple(
        pl.pallas_call(
            settle,
            out_shape=(out, out, out, out),
            in_specs=[anywhere] * 4,
            out_specs=(anywhere,) * 4,
            scratch_shapes=[pltpu.SemaphoreType.DMA((4,))],
            compiler_params=pltpu.CompilerParams(vmem_limit_bytes=2 * 1024 * 1024),
        )(*packed)
    )


def solution(mesh):
    spec = P(("groups", "dp"), "mp", None)
    return jax.shard_map(
        functools.partial(local, mesh.shape["mp"]),
        mesh=mesh,
        in_specs=(spec, spec, spec, spec, spec, P(("groups", "dp"), "mp")),
        out_specs=(spec, spec, spec, spec),
        check_vma=False,
    )
```
